128 devices in a mesh: node: 16 (over z, y), local: 8 (over x, core).
Axes of the slice: x: 4, y: 4, z: 4, core: 2. Of those that a mesh axis runs over, the one named last changes fastest.
Arguments:
- tokens: bfloat16 [16384, 3584], P(('node', 'local')), may hold values from -6 to 6
- grad_out: bfloat16 [16384, 3584], P(('node', 'local')), may hold values from -6 to 6
- expert_ids: int32 [16384, 8], P(('node', 'local')), may hold values from 0 to 127, as said below
- gate_weights: float32 [16384, 8], P(('node', 'local')), may hold values from 0.08 to 0.8
- w_gate: bfloat16 [128, 3584, 1024], P(('node', 'local')), may hold values from -0.09375 to 0.09375
- w_up: bfloat16 [128, 3584, 1024], P(('node', 'local')), may hold values from -0.09375 to 0.09375
- w_down: bfloat16 [128, 1024, 3584], P(('node', 'local')), may hold values from -0.09375 to 0.09375
Outputs:
- token_grads: bfloat16 [16384, 3584], P(('node', 'local'))
The draws below stay inside these ranges and needn't reach their ends.
Inputs may be any that keep to these rules, and one draw needn't show every extreme that they name: `expert_ids`: each row names 8 different experts; expert e belongs to node group e // 8, and the experts of one row lie in at most 4 node groups.
All inputs are finite; a program needn't handle non-finite values.
Results may differ from the reference program's by a relative error of at most 0.0057.
Values may be sent and summed in bfloat16 or wider, within the bound.
No kernel may reach another device: no remote copies, remote signals or barrier semaphores. Data moves between devices by JAX's collectives and lax.ppermute only.
A program may use at most 128 MiB of HBM per device.

```python
import math
import jax
import jax.numpy as jnp
from jax import lax

D = 3584
FF = 1024
TOP = 8
NODE_LIMIT = 4
TOK_DEV = 128
EXPERTS = 128
EXPERTS_NODE = 8
CAP = 6
TOKENS = 16384


def draw_expert_ids(key, part):
    key = jax.random.fold_in(key, 11)
    node_key, expert_key, order_key, shuffle_key = jax.random.split(key, 4)
    node_groups = EXPERTS // EXPERTS_NODE
    node_order = jax.random.permutation(order_key, node_groups).astype(jnp.int32)
    expert_order = jax.random.permutation(shuffle_key, EXPERTS).astype(jnp.int32)
    node_noise = jax.random.randint(node_key, (TOKENS, node_groups), 0, 65536, dtype=jnp.int32)
    node_score = (node_noise + node_order[None, :] * (32768 // node_groups)) * node_groups + jnp.arange(node_groups, dtype=jnp.int32)[None, :]
    picked_nodes = lax.top_k(node_score, NODE_LIMIT)[1].astype(jnp.int32)
    expert_node = jnp.arange(EXPERTS, dtype=jnp.int32) // EXPERTS_NODE
    member = jnp.any(picked_nodes[:, :, None] == expert_node[None, None, :], axis=1)
    expert_noise = jax.random.randint(expert_key, (TOKENS, EXPERTS), 0, 65536, dtype=jnp.int32)
    expert_score = (expert_noise + expert_order[None, :] * (32768 // EXPERTS)) * EXPERTS + jnp.arange(EXPERTS, dtype=jnp.int32)[None, :]
    expert_score = jnp.where(member, expert_score, -1 - jnp.arange(EXPERTS, dtype=jnp.int32)[None, :])
    return lax.top_k(expert_score, TOP)[1].astype(jnp.int32)


def steps_of(own_key, extent, cuts, least, high):
    factor_of, own = 1.0, jax.random.fold_in(own_key, 6)
    for dim, blocks in cuts:
        steps = jnp.exp(jax.random.uniform(jax.random.fold_in(own, dim), (blocks,), jnp.float32, least / len(cuts), high / len(cuts)))
        factor_of = factor_of * jnp.repeat(steps, extent[dim] // blocks).reshape([-1 if axis == dim else 1 for axis in range(len(extent))])
    return factor_of


def scatter_about(rng, dims, deviation, reach, shards=(), held_as=jnp.bfloat16):
    drawn = deviation * jax.random.normal(rng, dims, jnp.float32)
    if shards:
        drawn = drawn * steps_of(rng, dims, shards, -0.22, 0.18)
    return jnp.clip(drawn, -reach, reach).astype(held_as)


def setup_inputs(seed: int = 0) -> dict:
    arg_keys = jax.random.split(jax.random.key(seed), 8)
    tokens = scatter_about(arg_keys[0], (TOKENS, D), 1.0, 6.0, ((0, 128),))
    grad_out = scatter_about(arg_keys[1], (TOKENS, D), 1.0, 6.0, ((0, 128),))
    expert_ids = draw_expert_ids(jax.random.fold_in(arg_keys[7], 71), 0)
    gate_weights = jnp.clip(jnp.exp(math.log(0.8) - 2.3025851 * jax.random.uniform(arg_keys[3], (TOKENS, TOP), jnp.float32) ** steps_of(arg_keys[3], (TOKENS, TOP), ((0, 128),), -0.2, 0.2)), 0.08, 0.8)
    w_gate = scatter_about(arg_keys[4], (EXPERTS, D, FF), D ** -0.5, 0.09375, ((0, 128),))
    w_up = scatter_about(arg_keys[5], (EXPERTS, D, FF), D ** -0.5, 0.09375, ((0, 128),))
    w_down = scatter_about(arg_keys[6], (EXPERTS, FF, D), D ** -0.5, 0.09375, ((0, 128),))
    return dict(tokens=tokens, grad_out=grad_out, expert_ids=expert_ids, gate_weights=gate_weights, w_gate=w_gate, w_up=w_up, w_down=w_down)


def expert_grad(inputs, upstream, gate_matrix, up_matrix, down_matrix):
    gate_pre = jnp.dot(inputs, gate_matrix, preferred_element_type=jnp.float32)
    up_pre = jnp.dot(inputs, up_matrix, preferred_element_type=jnp.float32)
    hidden_grad = lax.dot_general(upstream, down_matrix, (((1,), (1,)), ((), ())), preferred_element_type=jnp.float32)
    sigmoid_gate = jax.nn.sigmoid(gate_pre)
    up_grad = (hidden_grad * gate_pre * sigmoid_gate).astype(jnp.bfloat16)
    gate_grad = (hidden_grad * up_pre * sigmoid_gate * (1.0 + gate_pre * (1.0 - sigmoid_gate))).astype(jnp.bfloat16)
    summed = jnp.dot(gate_grad, gate_matrix.T, preferred_element_type=jnp.float32)
    summed = summed + jnp.dot(up_grad, up_matrix.T, preferred_element_type=jnp.float32)
    return summed.astype(jnp.bfloat16)

def reference(tokens, grad_out, expert_ids, gate_weights, w_gate, w_up, w_down):
    blocks = TOKENS // TOK_DEV
    routes = expert_ids.reshape(blocks, TOK_DEV * TOP)
    onehot = (routes[:, :, None] == jnp.arange(EXPERTS, dtype=jnp.int32)[None, None, :]).astype(jnp.int32)
    route_rank = lax.optimization_barrier(jnp.sum((jnp.cumsum(onehot, axis=1) - onehot) * onehot, axis=2))
    kept_route = route_rank < CAP
    block_index = jnp.arange(blocks, dtype=jnp.int32)[:, None]
    token_index = block_index * TOK_DEV + jnp.arange(TOK_DEV * TOP, dtype=jnp.int32)[None, :] // TOP
    table_size = EXPERTS * blocks * CAP
    position = jnp.where(kept_route, (routes * blocks + block_index) * CAP + route_rank, table_size)
    position = position.reshape(-1).astype(jnp.int32)
    token_table = jnp.full((table_size,), TOKENS, jnp.int32).at[position].set(token_index.reshape(-1).astype(jnp.int32), mode='drop')
    gate_table = jnp.zeros((table_size,), jnp.float32).at[position].set(gate_weights.reshape(-1), mode='drop')
    token_table = token_table.reshape(EXPERTS, blocks * CAP)
    gate_table = gate_table.reshape(EXPERTS, blocks * CAP)
    padded_tokens = jnp.concatenate([tokens, jnp.zeros((1, D), tokens.dtype)], axis=0)
    padded_grads = jnp.concatenate([grad_out, jnp.zeros((1, D), grad_out.dtype)], axis=0)

    def one_expert(accumulated, operands):
        row_index, weights, gate_matrix, up_matrix, down_matrix = operands
        grads = expert_grad(padded_tokens[row_index], padded_grads[row_index], gate_matrix, up_matrix, down_matrix)
        accumulated = accumulated.at[row_index].add(weights[:, None] * grads.astype(jnp.float32), mode='drop')
        return (accumulated, None)
    accumulated, _ = lax.scan(one_expert, jnp.zeros((TOKENS, D), jnp.float32), (token_table, gate_table, w_gate, w_up, w_down))
    return accumulated.astype(jnp.bfloat16)
```

```python
import functools

import jax
import jax.numpy as jnp
from jax import lax
from jax.experimental import pallas as pl
from jax.experimental.pallas import tpu as pltpu
from jax.sharding import PartitionSpec as P

AXES = ("node", "local")
D = 3584
FF = 1024
TOP = 8
TOK = 128
EXPERTS = 128
UNIT = 896
GROUP = 256
SRC = 32
MIB = 1 << 20

PARTS = ((4, 0), (2, 4))


def iota(shape, dim):
    return lax.broadcasted_iota(jnp.int32, shape, dim)


def one(mask):
    return jnp.where(mask, 1.0, 0.0)


def ranked(ids):
    lanes = iota((TOK, EXPERTS), 1)
    chosen = jnp.zeros((TOK, EXPERTS), jnp.float32)
    for k in range(TOP):
        chosen = chosen + one(ids[:, k : k + 1] == lanes)
    earlier = one(iota((TOK, TOK), 1) < iota((TOK, TOK), 0))
    rank = jnp.dot(
        earlier.astype(jnp.bfloat16), chosen.astype(jnp.bfloat16), preferred_element_type=jnp.float32
    )
    return jnp.where(chosen > 0.5, rank, 64.0)


def pack_kernel(c, first, ids_ref, *refs):
    chunks = 8 // c
    x_refs, out_ref, onehot = refs[:chunks], refs[chunks], refs[chunks + 1]

    @pl.when(pl.program_id(0) == 0)
    def _():
        rank = ranked(ids_ref[...]).T.astype(jnp.bfloat16)
        rows = EXPERTS * 8
        spread = one(iota((rows, EXPERTS), 0) // 8 == iota((rows, EXPERTS), 1)).astype(jnp.bfloat16)
        rank = jnp.dot(spread, rank, preferred_element_type=jnp.float32).astype(jnp.int32)
        r = iota((rows, TOK), 0) % 8
        hit = rank == first + r % c
        for a in range(chunks):
            onehot[:, a * TOK : (a + 1) * TOK] = one(hit & (r // c == a)).astype(jnp.bfloat16)

    x = jnp.concatenate([ref[...] for ref in x_refs], axis=0)
    out_ref[...] = jnp.dot(onehot[...], x, preferred_element_type=jnp.float32).astype(jnp.bfloat16)


def pack(c, first, ids, tokens, grads):
    chunks = 8 // c
    specs, operands = [pl.BlockSpec((TOK, TOP), lambda i: (0, 0))], [ids]
    for a in range(chunks):
        start = a % (chunks // 2) * c
        specs.append(pl.BlockSpec((TOK, UNIT), lambda i, start=start: (0, start + i)))
        operands.append(tokens if a < chunks // 2 else grads)
    rows = EXPERTS * 8
    return pl.pallas_call(
        functools.partial(pack_kernel, c, first),
        grid=(c,),
        in_specs=specs,
        out_specs=pl.BlockSpec((rows, UNIT), lambda i: (0, i)),
        out_shape=jax.ShapeDtypeStruct((rows, c * UNIT), jnp.bfloat16),
        scratch_shapes=[pltpu.VMEM((rows, chunks * TOK), jnp.bfloat16)],
        compiler_params=pltpu.CompilerParams(vmem_limit_bytes=20 * MIB),
        cost_estimate=pl.CostEstimate(
            flops=2 * rows * chunks * TOK * c * UNIT, bytes_accessed=rows * c * UNIT * 2, transcendentals=0
        ),
        name="pack_slots",
    )(*operands)


def sorter(c):
    row, col = iota((GROUP, GROUP), 0), iota((GROUP, GROUP), 1)
    per_chunk = SRC * c
    inner = row % per_chunk
    return one(col == inner // c * 8 + row // per_chunk * c + inner % c).astype(jnp.bfloat16)


def unsorter(c):
    row, col = iota((GROUP, GROUP), 1), iota((GROUP, GROUP), 0)
    per_chunk = SRC * c
    inner = row % per_chunk
    return one(col == inner // c * 8 + row // per_chunk * c + inner % c).astype(jnp.bfloat16)


def ffn_kernel(c, out_at, wire_ref, wg_hbm, wu_hbm, wd_hbm, *refs):
    if out_at:
        refs = refs[1:]
    out_hbm, wg, wu, wd, x, up_g, gate_g, res, out, sems, out_sem = refs
    chunks, per_chunk = 8 // c, SRC * c
    width = c * UNIT
    step = 256
    blocks = FF // step

    def loads(j):
        cols = pl.ds(pl.multiple_of(j * step, step), step)
        return (
            pltpu.make_async_copy(wg_hbm.at[:, cols], wg.at[:, cols], sems.at[0, j]),
            pltpu.make_async_copy(wu_hbm.at[:, cols], wu.at[:, cols], sems.at[1, j]),
            pltpu.make_async_copy(wd_hbm.at[cols, :], wd.at[cols, :], sems.at[2, j]),
        )

    for j in range(blocks):
        for copy in loads(j):
            copy.start()

    sort = sorter(c)

    @pl.loop(0, EXPERTS // SRC)
    def _(g):
        rows_in = pl.ds(pl.multiple_of(g * GROUP, GROUP), GROUP)
        rows_x = pl.ds(pl.multiple_of(g * per_chunk, per_chunk), per_chunk)
        for u in range(c):
            part = jnp.dot(
                sort, wire_ref[rows_in, u * UNIT : (u + 1) * UNIT], preferred_element_type=jnp.float32
            ).astype(jnp.bfloat16)
            for a in range(chunks):
                at = a * width + u * UNIT
                x[rows_x, at : at + UNIT] = part[a * per_chunk : (a + 1) * per_chunk]

    @pl.loop(0, blocks)
    def _(j):
        for copy in loads(j):
            copy.wait()
        cols = pl.ds(pl.multiple_of(j * step, step), step)
        gate_pre = jnp.dot(x[:, :D], wg[:, cols], preferred_element_type=jnp.float32)
        up_pre = jnp.dot(x[:, :D], wu[:, cols], preferred_element_type=jnp.float32)
        hidden = lax.dot_general(
            x[:, D:], wd[cols, :], (((1,), (1,)), ((), ())), preferred_element_type=jnp.float32
        )
        s = jax.nn.sigmoid(gate_pre)
        up_g[:, cols] = (hidden * gate_pre * s).astype(jnp.bfloat16)
        gate_g[:, cols] = (hidden * up_pre * s * (1.0 + gate_pre * (1.0 - s))).astype(jnp.bfloat16)

    @pl.loop(0, D // 512)
    def _(j):
        cols = pl.ds(pl.multiple_of(j * 512, 512), 512)
        nt = (((1,), (1,)), ((), ()))
        total = lax.dot_general(gate_g[...], wg[cols, :], nt, preferred_element_type=jnp.float32)
        total = total + lax.dot_general(up_g[...], wu[cols, :], nt, preferred_element_type=jnp.float32)
        res[:, cols] = total.astype(jnp.bfloat16)

    unsort = unsorter(c)
    back = width // 2

    @pl.loop(0, EXPERTS // SRC)
    def _(g):
        rows_out = pl.ds(pl.multiple_of(g * GROUP, GROUP), GROUP)
        rows_x = pl.ds(pl.multiple_of(g * per_chunk, per_chunk), per_chunk)
        stack = jnp.concatenate([res[rows_x, a * back : (a + 1) * back] for a in range(chunks)], axis=0)
        out[rows_out, :] = jnp.dot(unsort, stack, preferred_element_type=jnp.float32).astype(jnp.bfloat16)

    done = pltpu.make_async_copy(out, out_hbm.at[:, pl.ds(out_at, back)], out_sem)
    done.start()
    done.wait()


def ffn(c, out_at, wire, w_gate, w_up, w_down, result=None):
    rows, back = EXPERTS * c, c * UNIT // 2
    wire_rows = EXPERTS * 8
    any_spec = pl.BlockSpec(memory_space=pl.ANY)
    operands = [wire, w_gate, w_up, w_down] + ([] if result is None else [result])
    return pl.pallas_call(
        functools.partial(ffn_kernel, c, out_at),
        in_specs=[pl.BlockSpec(memory_space=pltpu.VMEM)] + [any_spec] * (len(operands) - 1),
        out_specs=any_spec,
        out_shape=jax.ShapeDtypeStruct((wire_rows, 3 * UNIT), jnp.bfloat16),
        input_output_aliases={} if result is None else {4: 0},
        scratch_shapes=[
            pltpu.VMEM((D, FF), jnp.bfloat16),
            pltpu.VMEM((D, FF), jnp.bfloat16),
            pltpu.VMEM((FF, D), jnp.bfloat16),
            pltpu.VMEM((rows, 2 * D), jnp.bfloat16),
            pltpu.VMEM((rows, FF), jnp.bfloat16),
            pltpu.VMEM((rows, FF), jnp.bfloat16),
            pltpu.VMEM((rows, D), jnp.bfloat16),
            pltpu.VMEM((wire_rows, back), jnp.bfloat16),
            pltpu.SemaphoreType.DMA((3, 4)),
            pltpu.SemaphoreType.DMA,
        ],
        compiler_params=pltpu.CompilerParams(vmem_limit_bytes=54 * MIB),
        cost_estimate=pl.CostEstimate(
            flops=2 * rows * 5 * D * FF, bytes_accessed=3 * D * FF * 2, transcendentals=rows * FF
        ),
        name="expert_gradients",
    )(*operands)


def combine_kernel(ids_ref, weight_ref, y_ref, out_ref):
    ids, weight = ids_ref[...], weight_ref[...]
    lanes = iota((TOK, EXPERTS), 1)
    dense = jnp.zeros((TOK, EXPERTS), jnp.float32)
    for k in range(TOP):
        dense = dense + jnp.where(ids[:, k : k + 1] == lanes, weight[:, k : k + 1], 0.0)
    rows = EXPERTS * 8
    spread = one(iota((EXPERTS, rows), 1) // 8 == iota((EXPERTS, rows), 0)).astype(jnp.bfloat16)
    high = dense.astype(jnp.bfloat16)
    low = (dense - high.astype(jnp.float32)).astype(jnp.bfloat16)
    rank = ranked(ids).astype(jnp.bfloat16)
    rank, high, low = (
        jnp.dot(v, spread, preferred_element_type=jnp.float32) for v in (rank, high, low)
    )
    rank = rank.astype(jnp.int32)
    r = iota((TOK, rows), 1) % 8
    both = jnp.concatenate([high, low], axis=0)

    def weights(c, first, a):
        keep = (rank == first + r % c) & (r // c == a)
        keep = jnp.concatenate([keep, keep], axis=0)
        return jnp.where(keep, both, 0.0).astype(jnp.bfloat16)

    for h in range(2):
        four = weights(4, 0, h)
        for half in range(2):
            q = 2 * h + half
            total = jnp.dot(four, y_ref[:, half * UNIT : (half + 1) * UNIT], preferred_element_type=jnp.float32)
            total = total + jnp.dot(
                weights(2, 4, q), y_ref[:, 2 * UNIT : 3 * UNIT], preferred_element_type=jnp.float32
            )
            out_ref[:, q * UNIT : (q + 1) * UNIT] = (total[:TOK] + total[TOK:]).astype(jnp.bfloat16)


def combine(ids, weight, y):
    vmem = pl.BlockSpec(memory_space=pltpu.VMEM)
    return pl.pallas_call(
        combine_kernel,
        in_specs=[vmem] * 3,
        out_specs=vmem,
        out_shape=jax.ShapeDtypeStruct((TOK, D), jnp.bfloat16),
        compiler_params=pltpu.CompilerParams(vmem_limit_bytes=32 * MIB),
        cost_estimate=pl.CostEstimate(
            flops=2 * 2 * TOK * 2 * EXPERTS * 8 * D, bytes_accessed=EXPERTS * 8 * 3 * UNIT * 2, transcendentals=0
        ),
        name="combine_routes",
    )(ids, weight, y)


def exchange(wire):
    blocks = wire.reshape(EXPERTS, 8, wire.shape[1])
    return lax.all_to_all(blocks, AXES, split_axis=0, concat_axis=0, tiled=True).reshape(wire.shape)


def shards(tokens, grad_out, expert_ids, gate_weights, w_gate, w_up, w_down):
    w_gate, w_up, w_down = w_gate[0], w_up[0], w_down[0]
    wires = [exchange(pack(c, first, expert_ids, tokens, grad_out)) for c, first in PARTS]
    result = ffn(4, 0, wires[0], w_gate, w_up, w_down)
    result = ffn(2, 2 * UNIT, wires[1], w_gate, w_up, w_down, result)
    return combine(expert_ids, gate_weights, exchange(result))


def solution(mesh):
    rows = P(AXES, None)
    experts = P(AXES, None, None)
    return jax.shard_map(
        shards,
        mesh=mesh,
        in_specs=(rows, rows, rows, rows, experts, experts, experts),
        out_specs=rows,
        check_vma=False,
    )
```

```python
import functools

import jax
import jax.numpy as jnp
from jax import lax
from jax.experimental import pallas as pl
from jax.experimental.pallas import tpu as pltpu
from jax.sharding import PartitionSpec as P

AXES = ("node", "local")
D = 3584
FF = 1024
TOP = 8
TOK = 128
EXPERTS = 128
UNIT = 896
GROUP = 256
SRC = 32
PACK, PACK2 = 512, 256
MIB = 1 << 20

PARTS = ((4, 0), (2, 4))


def iota(shape, dim):
    return lax.broadcasted_iota(jnp.int32, shape, dim)


def one(mask):
    return jnp.where(mask, 1.0, 0.0)


def routes(ids):
    rows = iota((EXPERTS, TOK), 0)
    chosen = jnp.zeros((EXPERTS, TOK), jnp.float32)
    for k in range(TOP):
        chosen = chosen + one(ids[k : k + 1, :] == rows)
    earlier = one(iota((TOK, TOK), 0) < iota((TOK, TOK), 1))
    rank = jnp.dot(
        chosen.astype(jnp.bfloat16), earlier.astype(jnp.bfloat16), preferred_element_type=jnp.float32
    )
    return jnp.where(chosen > 0.5, rank, 64.0)


def spread_rows(v):
    rows = EXPERTS * 8
    spread = one(iota((rows, EXPERTS), 0) >> 3 == iota((rows, EXPERTS), 1)).astype(jnp.bfloat16)
    return jnp.dot(spread, v.astype(jnp.bfloat16), preferred_element_type=jnp.float32)


def pack_kernel(ids_ref, tokens_hbm, grads_hbm, *refs):
    out_refs, (x, onehot, sems) = refs[: len(PARTS)], refs[len(PARTS) :]

    def loads(i):
        cols = pl.ds(i * PACK, PACK)
        return (
            pltpu.make_async_copy(tokens_hbm.at[:, cols], x.at[pl.ds(0, TOK), cols], sems.at[0, i]),
            pltpu.make_async_copy(grads_hbm.at[:, cols], x.at[pl.ds(TOK, TOK), cols], sems.at[1, i]),
        )

    for i in range(D // PACK):
        for copy in loads(i):
            copy.start()

    rank = spread_rows(routes(ids_ref[...]))
    r = iota((EXPERTS * 8, TOK), 0) & 7

    def hits(c, first):
        slot = (r & (c - 1)).astype(jnp.float32) + first
        chunk = jnp.where(rank == slot, r // c, -1)
        for a in range(8 // c):
            onehot[:, a * TOK : (a + 1) * TOK] = one(chunk == a).astype(jnp.bfloat16)

    (four, first), (two, second) = PARTS
    hits(four, first)
    for i in range(D // PACK):
        for copy in loads(i):
            copy.wait()
        cols = slice(i * PACK, (i + 1) * PACK)
        out_refs[0][:, cols] = jnp.dot(
            onehot[:, : 2 * TOK], x[:, cols], preferred_element_type=jnp.float32
        ).astype(jnp.bfloat16)
    hits(two, second)
    half = D // 2
    for i in range(half // PACK2):
        low, high = slice(i * PACK2, (i + 1) * PACK2), slice(half + i * PACK2, half + (i + 1) * PACK2)
        stack = [x[:TOK, low], x[:TOK, high], x[TOK:, low], x[TOK:, high]]
        out_refs[1][:, low] = jnp.dot(
            onehot[...], jnp.concatenate(stack, axis=0), preferred_element_type=jnp.float32
        ).astype(jnp.bfloat16)


def in_hbm(v):
    return pltpu.with_memory_space_constraint(v, pltpu.HBM)


def pack(ids, tokens, grads):
    rows = EXPERTS * 8
    any_spec, vmem = pl.BlockSpec(memory_space=pl.ANY), pl.BlockSpec(memory_space=pltpu.VMEM)
    return pl.pallas_call(
        pack_kernel,
        in_specs=[vmem, any_spec, any_spec],
        out_specs=[vmem for _ in PARTS],
        out_shape=[jax.ShapeDtypeStruct((rows, c * UNIT), jnp.bfloat16) for c, _ in PARTS],
        scratch_shapes=[
            pltpu.VMEM((2 * TOK, D), jnp.bfloat16),
            pltpu.VMEM((rows, 4 * TOK), jnp.bfloat16),
            pltpu.SemaphoreType.DMA((2, D // PACK)),
        ],
        compiler_params=pltpu.CompilerParams(vmem_limit_bytes=24 * MIB),
        cost_estimate=pl.CostEstimate(
            flops=4 * rows * 2 * TOK * D, bytes_accessed=rows * 6 * UNIT * 2, transcendentals=0
        ),
        name="pack_slots",
    )(ids, in_hbm(tokens), in_hbm(grads))


def sorter(c):
    row, col = iota((GROUP, GROUP), 0), iota((GROUP, GROUP), 1)
    per_chunk = SRC * c
    inner = row % per_chunk
    return one(col == inner // c * 8 + row // per_chunk * c + inner % c).astype(jnp.bfloat16)


def unsorter(c):
    row, col = iota((GROUP, GROUP), 1), iota((GROUP, GROUP), 0)
    per_chunk = SRC * c
    inner = row % per_chunk
    return one(col == inner // c * 8 + row // per_chunk * c + inner % c).astype(jnp.bfloat16)


def ffn_kernel(c, wire_ref, wg_hbm, wu_hbm, wd_hbm, *refs):
    out_hbm, wg, wu, wd, x, up_g, gate_g, res, out, sems, out_sem = refs
    chunks, per_chunk = 8 // c, SRC * c
    width = c * UNIT
    step = 256
    blocks = FF // step

    def loads(j):
        cols = pl.ds(pl.multiple_of(j * step, step), step)
        return (
            pltpu.make_async_copy(wg_hbm.at[:, cols], wg.at[:, cols], sems.at[0, j]),
            pltpu.make_async_copy(wu_hbm.at[:, cols], wu.at[:, cols], sems.at[1, j]),
            pltpu.make_async_copy(wd_hbm.at[cols, :], wd.at[cols, :], sems.at[2, j]),
        )

    for j in range(blocks):
        for copy in loads(j):
            copy.start()

    sort = sorter(c)

    @pl.loop(0, EXPERTS // SRC)
    def _(g):
        rows_in = pl.ds(pl.multiple_of(g * GROUP, GROUP), GROUP)
        rows_x = pl.ds(pl.multiple_of(g * per_chunk, per_chunk), per_chunk)
        for u in range(c):
            part = jnp.dot(
                sort, wire_ref[rows_in, u * UNIT : (u + 1) * UNIT], preferred_element_type=jnp.float32
            ).astype(jnp.bfloat16)
            for a in range(chunks):
                at = a * width + u * UNIT
                x[rows_x, at : at + UNIT] = part[a * per_chunk : (a + 1) * per_chunk]

    @pl.loop(0, blocks)
    def _(j):
        for copy in loads(j):
            copy.wait()
        cols = pl.ds(pl.multiple_of(j * step, step), step)
        gate_pre = jnp.dot(x[:, :D], wg[:, cols], preferred_element_type=jnp.float32)
        up_pre = jnp.dot(x[:, :D], wu[:, cols], preferred_element_type=jnp.float32)
        hidden = lax.dot_general(
            x[:, D:], wd[cols, :], (((1,), (1,)), ((), ())), preferred_element_type=jnp.float32
        )
        s = jax.nn.sigmoid(gate_pre)
        up_g[:, cols] = (hidden * gate_pre * s).astype(jnp.bfloat16)
        gate_g[:, cols] = (hidden * up_pre * s * (1.0 + gate_pre * (1.0 - s))).astype(jnp.bfloat16)

    @pl.loop(0, D // 512)
    def _(j):
        cols = pl.ds(pl.multiple_of(j * 512, 512), 512)
        nt = (((1,), (1,)), ((), ()))
        total = lax.dot_general(gate_g[...], wg[cols, :], nt, preferred_element_type=jnp.float32)
        total = total + lax.dot_general(up_g[...], wu[cols, :], nt, preferred_element_type=jnp.float32)
        res[:, cols] = total.astype(jnp.bfloat16)

    unsort = unsorter(c)
    back = width // 2

    @pl.loop(0, EXPERTS // SRC)
    def _(g):
        rows_out = pl.ds(pl.multiple_of(g * GROUP, GROUP), GROUP)
        rows_x = pl.ds(pl.multiple_of(g * per_chunk, per_chunk), per_chunk)
        stack = jnp.concatenate([res[rows_x, a * back : (a + 1) * back] for a in range(chunks)], axis=0)
        out[rows_out, :] = jnp.dot(unsort, stack, preferred_element_type=jnp.float32).astype(jnp.bfloat16)

    done = pltpu.make_async_copy(out, out_hbm, out_sem)
    done.start()
    done.wait()


def ffn(c, wire, w_gate, w_up, w_down):
    rows, back = EXPERTS * c, c * UNIT // 2
    wire_rows = EXPERTS * 8
    any_spec = pl.BlockSpec(memory_space=pl.ANY)
    return pl.pallas_call(
        functools.partial(ffn_kernel, c),
        in_specs=[pl.BlockSpec(memory_space=pltpu.VMEM)] + [any_spec] * 3,
        out_specs=any_spec,
        out_shape=jax.ShapeDtypeStruct((wire_rows, back), jnp.bfloat16),
        scratch_shapes=[
            pltpu.VMEM((D, FF), jnp.bfloat16),
            pltpu.VMEM((D, FF), jnp.bfloat16),
            pltpu.VMEM((FF, D), jnp.bfloat16),
            pltpu.VMEM((rows, 2 * D), jnp.bfloat16),
            pltpu.VMEM((rows, FF), jnp.bfloat16),
            pltpu.VMEM((rows, FF), jnp.bfloat16),
            pltpu.VMEM((rows, D), jnp.bfloat16),
            pltpu.VMEM((wire_rows, back), jnp.bfloat16),
            pltpu.SemaphoreType.DMA((3, 4)),
            pltpu.SemaphoreType.DMA,
        ],
        compiler_params=pltpu.CompilerParams(vmem_limit_bytes=54 * MIB),
        cost_estimate=pl.CostEstimate(
            flops=2 * rows * 5 * D * FF, bytes_accessed=3 * D * FF * 2, transcendentals=rows * FF
        ),
        name="expert_gradients",
    )(wire, w_gate, w_up, w_down)


def spread_weights(ids, weight, c, first):
    rows = iota((EXPERTS, TOK), 0)
    dense = jnp.zeros((EXPERTS, TOK), jnp.float32)
    for k in range(TOP):
        dense = dense + jnp.where(ids[k : k + 1, :] == rows, weight[k : k + 1, :], 0.0)
    high = dense.astype(jnp.bfloat16).astype(jnp.float32)
    wide = EXPERTS * c
    spread = one(iota((wide, EXPERTS), 0) // c == iota((wide, EXPERTS), 1)).astype(jnp.bfloat16)
    rank, high, low = (
        jnp.dot(spread, v.astype(jnp.bfloat16), preferred_element_type=jnp.float32)
        for v in (routes(ids), high, dense - high)
    )
    hit = rank == (iota((wide, TOK), 0) % c).astype(jnp.float32) + first
    pair = [jnp.where(hit, v, 0.0).T for v in (high, low)]
    return jnp.concatenate(pair, axis=0).astype(jnp.bfloat16)


def slot_rows(c, y_ref, rows_ref):
    sort, per_chunk, back = sorter(c), SRC * c, c * UNIT // 2
    for g in range(EXPERTS // SRC):
        part = jnp.dot(
            sort, y_ref[g * GROUP : (g + 1) * GROUP, :], preferred_element_type=jnp.float32
        ).astype(jnp.bfloat16)
        for a in range(8 // c):
            rows_ref[g * per_chunk : (g + 1) * per_chunk, a * back : (a + 1) * back] = part[
                a * per_chunk : (a + 1) * per_chunk
            ]


def first_combine_kernel(ids_ref, weight_ref, y_ref, sum_ref, late_ref, rows_ref):
    ids, weight = ids_ref[...], weight_ref[...]
    late_ref[...] = spread_weights(ids, weight, *PARTS[1])
    slot_rows(4, y_ref, rows_ref)
    four = spread_weights(ids, weight, *PARTS[0])
    for q in range(4):
        cols = slice(q * UNIT, (q + 1) * UNIT)
        total = jnp.dot(four, rows_ref[:, cols], preferred_element_type=jnp.float32)
        sum_ref[:, cols] = total[:TOK] + total[TOK:]


def last_combine_kernel(late_ref, sum_hbm, y_ref, out_ref, sums, rows_ref, sem):
    copy = pltpu.make_async_copy(sum_hbm, sums, sem)
    copy.start()
    slot_rows(2, y_ref, rows_ref)
    copy.wait()
    for q in range(4):
        cols = slice(q * UNIT, (q + 1) * UNIT)
        total = jnp.dot(late_ref[...], rows_ref[:, cols], preferred_element_type=jnp.float32)
        out_ref[:, cols] = (sums[:, cols] + total[:TOK] + total[TOK:]).astype(jnp.bfloat16)


def first_combine(ids, weight, y):
    vmem = pl.BlockSpec(memory_space=pltpu.VMEM)
    c, late = PARTS[0][0], PARTS[1][0]
    return pl.pallas_call(
        first_combine_kernel,
        in_specs=[vmem] * 3,
        out_specs=(vmem, vmem),
        out_shape=(
            pltpu.HBM((TOK, D), jnp.float32),
            pltpu.VMEM((2 * TOK, EXPERTS * late), jnp.bfloat16),
        ),
        scratch_shapes=[pltpu.VMEM((EXPERTS * c, D), jnp.bfloat16)],
        compiler_params=pltpu.CompilerParams(vmem_limit_bytes=40 * MIB),
        cost_estimate=pl.CostEstimate(
            flops=2 * 2 * TOK * EXPERTS * c * D * 2, bytes_accessed=EXPERTS * c * D * 2, transcendentals=0
        ),
        name="combine_first_slots",
    )(ids, weight, y)


def last_combine(late, sums, y):
    vmem = pl.BlockSpec(memory_space=pltpu.VMEM)
    c = PARTS[1][0]
    return pl.pallas_call(
        last_combine_kernel,
        in_specs=[vmem, pl.BlockSpec(memory_space=pl.ANY), vmem],
        out_specs=vmem,
        out_shape=jax.ShapeDtypeStruct((TOK, D), jnp.bfloat16),
        scratch_shapes=[
            pltpu.VMEM((TOK, D), jnp.float32),
            pltpu.VMEM((EXPERTS * c, D), jnp.bfloat16),
            pltpu.SemaphoreType.DMA,
        ],
        compiler_params=pltpu.CompilerParams(vmem_limit_bytes=20 * MIB),
        cost_estimate=pl.CostEstimate(
            flops=2 * 2 * TOK * EXPERTS * c * D * 2, bytes_accessed=EXPERTS * c * D * 2, transcendentals=0
        ),
        name="combine_last_slots",
    )(late, in_hbm(sums), y)


def exchange(wire):
    blocks = wire.reshape(EXPERTS, 8, wire.shape[1])
    return lax.all_to_all(blocks, AXES, split_axis=0, concat_axis=0, tiled=True).reshape(wire.shape)


def shards(tokens, grad_out, expert_ids, gate_weights, w_gate, w_up, w_down):
    w_gate, w_up, w_down = w_gate[0], w_up[0], w_down[0]
    ids, weights = expert_ids.T, gate_weights.T
    returned = []
    for (c, _), wire in zip(PARTS, pack(ids, tokens, grad_out)):
        returned.append(exchange(ffn(c, exchange(wire), w_gate, w_up, w_down)))
    sums, late = first_combine(ids, weights, returned[0])
    return last_combine(late, sums, returned[1])


def solution(mesh):
    rows = P(AXES, None)
    experts = P(AXES, None, None)
    return jax.shard_map(
        shards,
        mesh=mesh,
        in_specs=(rows, rows, rows, rows, experts, experts, experts),
        out_specs=rows,
        check_vma=False,
    )
```

```python
import functools

import jax
import jax.numpy as jnp
from jax import lax
from jax.experimental import pallas as pl
from jax.experimental.pallas import tpu as pltpu
from jax.sharding import PartitionSpec as P

AXES = ("node", "local")
D = 3584
FF = 1024
TOP = 8
TOK = 128
EXPERTS = 128
UNIT = 896
GROUP = 256
SRC = 32
MIB = 1 << 20

PARTS = ((4, 0), (2, 4))


def iota(shape, dim):
    return lax.broadcasted_iota(jnp.int32, shape, dim)


def one(mask):
    return jnp.where(mask, 1.0, 0.0)


def routes(ids):
    rows = iota((EXPERTS, TOK), 0)
    chosen = jnp.zeros((EXPERTS, TOK), jnp.float32)
    for k in range(TOP):
        chosen = chosen + one(ids[k : k + 1, :] == rows)
    earlier = one(iota((TOK, TOK), 0) < iota((TOK, TOK), 1))
    rank = jnp.dot(
        chosen.astype(jnp.bfloat16), earlier.astype(jnp.bfloat16), preferred_element_type=jnp.float32
    )
    return jnp.where(chosen > 0.5, rank, 64.0)


def spread_rows(v):
    rows = EXPERTS * 8
    spread = one(iota((rows, EXPERTS), 0) >> 3 == iota((rows, EXPERTS), 1)).astype(jnp.bfloat16)
    return jnp.dot(spread, v.astype(jnp.bfloat16), preferred_element_type=jnp.float32)


def pack_kernel(ids_hbm, tokens_hbm, grads_hbm, *refs):
    out_refs, (ids, x, onehot, sems) = refs[: len(PARTS)], refs[len(PARTS) :]

    load_ids = pltpu.make_async_copy(ids_hbm, ids, sems.at[2])
    load_ids.start()
    loads = (
        pltpu.make_async_copy(tokens_hbm, x.at[pl.ds(0, TOK), :], sems.at[0]),
        pltpu.make_async_copy(grads_hbm, x.at[pl.ds(TOK, TOK), :], sems.at[1]),
    )
    for copy in loads:
        copy.start()

    load_ids.wait()
    rank = spread_rows(routes(ids[...]))
    r = iota((EXPERTS * 8, TOK), 0) & 7

    def hits(c, first):
        slot = (r & (c - 1)).astype(jnp.float32) + first
        chunk = jnp.where(rank == slot, r // c, -1)
        for a in range(8 // c):
            onehot[:, a * TOK : (a + 1) * TOK] = one(chunk == a).astype(jnp.bfloat16)

    (four, first), (two, second) = PARTS
    hits(four, first)
    for copy in loads:
        copy.wait()
    half = D // 2

    @pl.loop(0, 2)
    def _(i):
        cols = pl.ds(pl.multiple_of(i * half, half), half)
        out_refs[0][:, cols] = jnp.dot(
            onehot[:, : 2 * TOK], x[:, cols], preferred_element_type=jnp.float32
        ).astype(jnp.bfloat16)

    hits(two, second)

    @pl.loop(0, 2)
    def _(i):
        low = pl.ds(pl.multiple_of(i * UNIT, UNIT), UNIT)
        high = pl.ds(pl.multiple_of(half + i * UNIT, UNIT), UNIT)
        stack = [x[:TOK, low], x[:TOK, high], x[TOK:, low], x[TOK:, high]]
        out_refs[1][:, low] = jnp.dot(
            onehot[...], jnp.concatenate(stack, axis=0), preferred_element_type=jnp.float32
        ).astype(jnp.bfloat16)


def in_hbm(v):
    return pltpu.with_memory_space_constraint(v, pltpu.HBM)


def pack(ids, tokens, grads):
    rows = EXPERTS * 8
    any_spec, vmem = pl.BlockSpec(memory_space=pl.ANY), pl.BlockSpec(memory_space=pltpu.VMEM)
    return pl.pallas_call(
        pack_kernel,
        in_specs=[any_spec] * 3,
        out_specs=[vmem for _ in PARTS],
        out_shape=[jax.ShapeDtypeStruct((rows, c * UNIT), jnp.bfloat16) for c, _ in PARTS],
        scratch_shapes=[
            pltpu.VMEM((TOP, TOK), jnp.int32),
            pltpu.VMEM((2 * TOK, D), jnp.bfloat16),
            pltpu.VMEM((rows, 4 * TOK), jnp.bfloat16),
            pltpu.SemaphoreType.DMA((3,)),
        ],
        compiler_params=pltpu.CompilerParams(vmem_limit_bytes=24 * MIB),
        cost_estimate=pl.CostEstimate(
            flops=4 * rows * 2 * TOK * D, bytes_accessed=rows * 6 * UNIT * 2, transcendentals=0
        ),
        name="pack_slots",
    )(in_hbm(ids), in_hbm(tokens), in_hbm(grads))


def sorter(c):
    row, col = iota((GROUP, GROUP), 0), iota((GROUP, GROUP), 1)
    per_chunk = SRC * c
    inner = row % per_chunk
    return one(col == inner // c * 8 + row // per_chunk * c + inner % c).astype(jnp.bfloat16)


def unsorter(c):
    row, col = iota((GROUP, GROUP), 1), iota((GROUP, GROUP), 0)
    per_chunk = SRC * c
    inner = row % per_chunk
    return one(col == inner // c * 8 + row // per_chunk * c + inner % c).astype(jnp.bfloat16)


def ffn_kernel(c, wire_ref, wg_hbm, wu_hbm, wd_hbm, *refs):
    out_hbm, wg, wu, wd, x, up_g, gate_g, res, out, sems, out_sem = refs
    chunks, per_chunk = 8 // c, SRC * c
    width = c * UNIT
    step = 256
    blocks = FF // step

    def loads(j):
        cols = pl.ds(pl.multiple_of(j * step, step), step)
        return (
            pltpu.make_async_copy(wg_hbm.at[:, cols], wg.at[:, cols], sems.at[0, j]),
            pltpu.make_async_copy(wu_hbm.at[:, cols], wu.at[:, cols], sems.at[1, j]),
            pltpu.make_async_copy(wd_hbm.at[cols, :], wd.at[cols, :], sems.at[2, j]),
        )

    for j in range(blocks):
        for copy in loads(j):
            copy.start()

    sort = sorter(c)

    @pl.loop(0, EXPERTS // SRC)
    def _(g):
        rows_in = pl.ds(pl.multiple_of(g * GROUP, GROUP), GROUP)
        rows_x = pl.ds(pl.multiple_of(g * per_chunk, per_chunk), per_chunk)
        for u in range(c):
            part = jnp.dot(
                sort, wire_ref[rows_in, u * UNIT : (u + 1) * UNIT], preferred_element_type=jnp.float32
            ).astype(jnp.bfloat16)
            for a in range(chunks):
                at = a * width + u * UNIT
                x[rows_x, at : at + UNIT] = part[a * per_chunk : (a + 1) * per_chunk]

    @pl.loop(0, blocks)
    def _(j):
        for copy in loads(j):
            copy.wait()
        cols = pl.ds(pl.multiple_of(j * step, step), step)
        gate_pre = jnp.dot(x[:, :D], wg[:, cols], preferred_element_type=jnp.float32)
        up_pre = jnp.dot(x[:, :D], wu[:, cols], preferred_element_type=jnp.float32)
        hidden = lax.dot_general(
            x[:, D:], wd[cols, :], (((1,), (1,)), ((), ())), preferred_element_type=jnp.float32
        )
        s = jax.nn.sigmoid(gate_pre)
        up_g[:, cols] = (hidden * gate_pre * s).astype(jnp.bfloat16)
        gate_g[:, cols] = (hidden * up_pre * s * (1.0 + gate_pre * (1.0 - s))).astype(jnp.bfloat16)

    @pl.loop(0, D // 512)
    def _(j):
        cols = pl.ds(pl.multiple_of(j * 512, 512), 512)
        nt = (((1,), (1,)), ((), ()))
        total = lax.dot_general(gate_g[...], wg[cols, :], nt, preferred_element_type=jnp.float32)
        total = total + lax.dot_general(up_g[...], wu[cols, :], nt, preferred_element_type=jnp.float32)
        res[:, cols] = total.astype(jnp.bfloat16)

    unsort = unsorter(c)
    back = width // 2

    @pl.loop(0, EXPERTS // SRC)
    def _(g):
        rows_out = pl.ds(pl.multiple_of(g * GROUP, GROUP), GROUP)
        rows_x = pl.ds(pl.multiple_of(g * per_chunk, per_chunk), per_chunk)
        stack = jnp.concatenate([res[rows_x, a * back : (a + 1) * back] for a in range(chunks)], axis=0)
        out[rows_out, :] = jnp.dot(unsort, stack, preferred_element_type=jnp.float32).astype(jnp.bfloat16)

    done = pltpu.make_async_copy(out, out_hbm, out_sem)
    done.start()
    done.wait()


def ffn(c, wire, w_gate, w_up, w_down):
    rows, back = EXPERTS * c, c * UNIT // 2
    wire_rows = EXPERTS * 8
    any_spec = pl.BlockSpec(memory_space=pl.ANY)
    return pl.pallas_call(
        functools.partial(ffn_kernel, c),
        in_specs=[pl.BlockSpec(memory_space=pltpu.VMEM)] + [any_spec] * 3,
        out_specs=any_spec,
        out_shape=jax.ShapeDtypeStruct((wire_rows, back), jnp.bfloat16),
        scratch_shapes=[
            pltpu.VMEM((D, FF), jnp.bfloat16),
            pltpu.VMEM((D, FF), jnp.bfloat16),
            pltpu.VMEM((FF, D), jnp.bfloat16),
            pltpu.VMEM((rows, 2 * D), jnp.bfloat16),
            pltpu.VMEM((rows, FF), jnp.bfloat16),
            pltpu.VMEM((rows, FF), jnp.bfloat16),
            pltpu.VMEM((rows, D), jnp.bfloat16),
            pltpu.VMEM((wire_rows, back), jnp.bfloat16),
            pltpu.SemaphoreType.DMA((3, 4)),
            pltpu.SemaphoreType.DMA,
        ],
        compiler_params=pltpu.CompilerParams(vmem_limit_bytes=54 * MIB),
        cost_estimate=pl.CostEstimate(
            flops=2 * rows * 5 * D * FF, bytes_accessed=3 * D * FF * 2, transcendentals=rows * FF
        ),
        name="expert_gradients",
    )(wire, w_gate, w_up, w_down)


def spread_weights(ids, weight, c, first):
    rows = iota((EXPERTS, TOK), 0)
    dense = jnp.zeros((EXPERTS, TOK), jnp.float32)
    for k in range(TOP):
        dense = dense + jnp.where(ids[k : k + 1, :] == rows, weight[k : k + 1, :], 0.0)
    high = dense.astype(jnp.bfloat16).astype(jnp.float32)
    wide = EXPERTS * c
    spread = one(iota((wide, EXPERTS), 0) // c == iota((wide, EXPERTS), 1)).astype(jnp.bfloat16)
    rank, high, low = (
        jnp.dot(spread, v.astype(jnp.bfloat16), preferred_element_type=jnp.float32)
        for v in (routes(ids), high, dense - high)
    )
    hit = rank == (iota((wide, TOK), 0) % c).astype(jnp.float32) + first
    pair = [jnp.where(hit, v, 0.0).T for v in (high, low)]
    return jnp.concatenate(pair, axis=0).astype(jnp.bfloat16)


def slot_rows(c, y_ref, rows_ref):
    sort, per_chunk, back = sorter(c), SRC * c, c * UNIT // 2
    for g in range(EXPERTS // SRC):
        part = jnp.dot(
            sort, y_ref[g * GROUP : (g + 1) * GROUP, :], preferred_element_type=jnp.float32
        ).astype(jnp.bfloat16)
        for a in range(8 // c):
            rows_ref[g * per_chunk : (g + 1) * per_chunk, a * back : (a + 1) * back] = part[
                a * per_chunk : (a + 1) * per_chunk
            ]


def first_combine_kernel(ids_ref, weight_ref, y_ref, sum_ref, late_ref, rows_ref):
    ids, weight = ids_ref[...], weight_ref[...]
    late_ref[...] = spread_weights(ids, weight, *PARTS[1])
    slot_rows(4, y_ref, rows_ref)
    four = spread_weights(ids, weight, *PARTS[0])
    for q in range(4):
        cols = slice(q * UNIT, (q + 1) * UNIT)
        total = jnp.dot(four, rows_ref[:, cols], preferred_element_type=jnp.float32)
        sum_ref[:, cols] = total[:TOK] + total[TOK:]


def last_combine_kernel(late_ref, sum_hbm, y_ref, out_ref, sums, rows_ref, sem):
    copy = pltpu.make_async_copy(sum_hbm, sums, sem)
    copy.start()
    slot_rows(2, y_ref, rows_ref)
    copy.wait()
    for q in range(4):
        cols = slice(q * UNIT, (q + 1) * UNIT)
        total = jnp.dot(late_ref[...], rows_ref[:, cols], preferred_element_type=jnp.float32)
        out_ref[:, cols] = (sums[:, cols] + total[:TOK] + total[TOK:]).astype(jnp.bfloat16)


def first_combine(ids, weight, y):
    vmem = pl.BlockSpec(memory_space=pltpu.VMEM)
    c, late = PARTS[0][0], PARTS[1][0]
    return pl.pallas_call(
        first_combine_kernel,
        in_specs=[vmem] * 3,
        out_specs=(vmem, vmem),
        out_shape=(
            pltpu.HBM((TOK, D), jnp.float32),
            pltpu.VMEM((2 * TOK, EXPERTS * late), jnp.bfloat16),
        ),
        scratch_shapes=[pltpu.VMEM((EXPERTS * c, D), jnp.bfloat16)],
        compiler_params=pltpu.CompilerParams(vmem_limit_bytes=40 * MIB),
        cost_estimate=pl.CostEstimate(
            flops=2 * 2 * TOK * EXPERTS * c * D * 2, bytes_accessed=EXPERTS * c * D * 2, transcendentals=0
        ),
        name="combine_first_slots",
    )(ids, weight, y)


def last_combine(late, sums, y):
    vmem = pl.BlockSpec(memory_space=pltpu.VMEM)
    c = PARTS[1][0]
    return pl.pallas_call(
        last_combine_kernel,
        in_specs=[vmem, pl.BlockSpec(memory_space=pl.ANY), vmem],
        out_specs=vmem,
        out_shape=jax.ShapeDtypeStruct((TOK, D), jnp.bfloat16),
        scratch_shapes=[
            pltpu.VMEM((TOK, D), jnp.float32),
            pltpu.VMEM((EXPERTS * c, D), jnp.bfloat16),
            pltpu.SemaphoreType.DMA,
        ],
        compiler_params=pltpu.CompilerParams(vmem_limit_bytes=20 * MIB),
        cost_estimate=pl.CostEstimate(
            flops=2 * 2 * TOK * EXPERTS * c * D * 2, bytes_accessed=EXPERTS * c * D * 2, transcendentals=0
        ),
        name="combine_last_slots",
    )(late, in_hbm(sums), y)


def exchange(wire):
    blocks = wire.reshape(EXPERTS, 8, wire.shape[1])
    return lax.all_to_all(blocks, AXES, split_axis=0, concat_axis=0, tiled=True).reshape(wire.shape)


def shards(tokens, grad_out, expert_ids, gate_weights, w_gate, w_up, w_down):
    w_gate, w_up, w_down = w_gate[0], w_up[0], w_down[0]
    ids, weights = expert_ids.T, gate_weights.T
    returned = []
    for (c, _), wire in zip(PARTS, pack(ids, tokens, grad_out)):
        returned.append(exchange(ffn(c, exchange(wire), w_gate, w_up, w_down)))
    sums, late = first_combine(ids, weights, returned[0])
    return last_combine(late, sums, returned[1])


def solution(mesh):
    rows = P(AXES, None)
    experts = P(AXES, None, None)
    return jax.shard_map(
        shards,
        mesh=mesh,
        in_specs=(rows, rows, rows, rows, experts, experts, experts),
        out_specs=rows,
        check_vma=False,
    )
```

```python
import functools

import jax
import jax.numpy as jnp
from jax import lax
from jax.experimental import pallas as pl
from jax.experimental.pallas import tpu as pltpu
from jax.sharding import PartitionSpec as P

AXES = ("node", "local")
D = 3584
FF = 1024
TOP = 8
TOK = 128
EXPERTS = 128
UNIT = 896
GROUP = 256
BLOCK = 512
SRC = 32
MIB = 1 << 20

PARTS = ((4, 0), (2, 4))


def iota(shape, dim):
    return lax.broadcasted_iota(jnp.int32, shape, dim)


def one(mask):
    return jnp.where(mask, 1.0, 0.0)


def routes(ids):
    rows = iota((EXPERTS, TOK), 0)
    chosen = jnp.zeros((EXPERTS, TOK), jnp.float32)
    for k in range(TOP):
        chosen = chosen + one(ids[k : k + 1, :] == rows)
    earlier = one(iota((TOK, TOK), 0) < iota((TOK, TOK), 1))
    rank = jnp.dot(
        chosen.astype(jnp.bfloat16), earlier.astype(jnp.bfloat16), preferred_element_type=jnp.float32
    )
    return jnp.where(chosen > 0.5, rank, 64.0)


def pack_kernel(ids_hbm, tokens_hbm, grads_hbm, *refs):
    out_refs, (ids, x, sems) = refs[: len(PARTS)], refs[len(PARTS) :]

    load_ids = pltpu.make_async_copy(ids_hbm, ids, sems.at[2])
    load_ids.start()
    loads = (
        pltpu.make_async_copy(tokens_hbm, x.at[pl.ds(0, TOK), :], sems.at[0]),
        pltpu.make_async_copy(grads_hbm, x.at[pl.ds(TOK, TOK), :], sems.at[1]),
    )
    for copy in loads:
        copy.start()

    load_ids.wait()
    ranks = routes(ids[...]).astype(jnp.bfloat16)
    spread = one(iota((BLOCK, BLOCK // 8), 0) >> 3 == iota((BLOCK, BLOCK // 8), 1)).astype(jnp.bfloat16)
    r = iota((BLOCK, TOK), 0) & 7
    blocks = EXPERTS * 8 // BLOCK

    def onehot(g, c, first):
        rank = ranks[g * BLOCK // 8 : (g + 1) * BLOCK // 8, :]
        rank = jnp.dot(spread, rank, preferred_element_type=jnp.float32)
        slot = (r & (c - 1)).astype(jnp.float32) + first
        chunk = jnp.where(rank == slot, r // c, -1)
        return jnp.concatenate([one(chunk == a).astype(jnp.bfloat16) for a in range(8 // c)], axis=1)

    def store(out_ref, g, hits, rows):
        out_ref[g * BLOCK : (g + 1) * BLOCK, :] = jnp.dot(
            hits, rows, preferred_element_type=jnp.float32
        ).astype(jnp.bfloat16)

    hits = onehot(0, *PARTS[0])
    for copy in loads:
        copy.wait()
    for g in range(blocks):
        store(out_refs[0], g, hits if g == 0 else onehot(g, *PARTS[0]), x[...])
    half = D // 2
    for g in range(blocks):
        stack = [x[:TOK, :half], x[:TOK, half:], x[TOK:, :half], x[TOK:, half:]]
        store(out_refs[1], g, onehot(g, *PARTS[1]), jnp.concatenate(stack, axis=0))


def in_hbm(v):
    return pltpu.with_memory_space_constraint(v, pltpu.HBM)


def pack(ids, tokens, grads):
    rows = EXPERTS * 8
    any_spec, vmem = pl.BlockSpec(memory_space=pl.ANY), pl.BlockSpec(memory_space=pltpu.VMEM)
    return pl.pallas_call(
        pack_kernel,
        in_specs=[any_spec] * 3,
        out_specs=[vmem for _ in PARTS],
        out_shape=[jax.ShapeDtypeStruct((rows, c * UNIT), jnp.bfloat16) for c, _ in PARTS],
        scratch_shapes=[
            pltpu.VMEM((TOP, TOK), jnp.int32),
            pltpu.VMEM((2 * TOK, D), jnp.bfloat16),
            pltpu.SemaphoreType.DMA((3,)),
        ],
        compiler_params=pltpu.CompilerParams(vmem_limit_bytes=24 * MIB),
        cost_estimate=pl.CostEstimate(
            flops=4 * rows * 2 * TOK * D, bytes_accessed=rows * 6 * UNIT * 2, transcendentals=0
        ),
        name="pack_slots",
    )(in_hbm(ids), in_hbm(tokens), in_hbm(grads))


def sorter(c):
    row, col = iota((GROUP, GROUP), 0), iota((GROUP, GROUP), 1)
    per_chunk = SRC * c
    inner = row % per_chunk
    return one(col == inner // c * 8 + row // per_chunk * c + inner % c).astype(jnp.bfloat16)


def unsorter(c):
    row, col = iota((GROUP, GROUP), 1), iota((GROUP, GROUP), 0)
    per_chunk = SRC * c
    inner = row % per_chunk
    return one(col == inner // c * 8 + row // per_chunk * c + inner % c).astype(jnp.bfloat16)


def ffn_kernel(c, wire_ref, wg_hbm, wu_hbm, wd_hbm, *refs):
    out_hbm, wg, wu, wd, x, up_g, gate_g, res, out, sems, out_sem = refs
    chunks, per_chunk = 8 // c, SRC * c
    width = c * UNIT
    step = 256
    blocks = FF // step

    def loads(j):
        cols = pl.ds(pl.multiple_of(j * step, step), step)
        return (
            pltpu.make_async_copy(wg_hbm.at[:, cols], wg.at[:, cols], sems.at[0, j]),
            pltpu.make_async_copy(wu_hbm.at[:, cols], wu.at[:, cols], sems.at[1, j]),
            pltpu.make_async_copy(wd_hbm.at[cols, :], wd.at[cols, :], sems.at[2, j]),
        )

    for j in range(blocks):
        for copy in loads(j):
            copy.start()

    sort = sorter(c)

    @pl.loop(0, EXPERTS // SRC)
    def _(g):
        rows_in = pl.ds(pl.multiple_of(g * GROUP, GROUP), GROUP)
        rows_x = pl.ds(pl.multiple_of(g * per_chunk, per_chunk), per_chunk)
        for u in range(c):
            part = jnp.dot(
                sort, wire_ref[rows_in, u * UNIT : (u + 1) * UNIT], preferred_element_type=jnp.float32
            ).astype(jnp.bfloat16)
            for a in range(chunks):
                at = a * width + u * UNIT
                x[rows_x, at : at + UNIT] = part[a * per_chunk : (a + 1) * per_chunk]

    @pl.loop(0, blocks)
    def _(j):
        for copy in loads(j):
            copy.wait()
        cols = pl.ds(pl.multiple_of(j * step, step), step)
        gate_pre = jnp.dot(x[:, :D], wg[:, cols], preferred_element_type=jnp.float32)
        up_pre = jnp.dot(x[:, :D], wu[:, cols], preferred_element_type=jnp.float32)
        hidden = lax.dot_general(
            x[:, D:], wd[cols, :], (((1,), (1,)), ((), ())), preferred_element_type=jnp.float32
        )
        s = jax.nn.sigmoid(gate_pre)
        up_g[:, cols] = (hidden * gate_pre * s).astype(jnp.bfloat16)
        gate_g[:, cols] = (hidden * up_pre * s * (1.0 + gate_pre * (1.0 - s))).astype(jnp.bfloat16)

    @pl.loop(0, D // 512)
    def _(j):
        cols = pl.ds(pl.multiple_of(j * 512, 512), 512)
        nt = (((1,), (1,)), ((), ()))
        total = lax.dot_general(gate_g[...], wg[cols, :], nt, preferred_element_type=jnp.float32)
        total = total + lax.dot_general(up_g[...], wu[cols, :], nt, preferred_element_type=jnp.float32)
        res[:, cols] = total.astype(jnp.bfloat16)

    unsort = unsorter(c)
    back = width // 2

    @pl.loop(0, EXPERTS // SRC)
    def _(g):
        rows_out = pl.ds(pl.multiple_of(g * GROUP, GROUP), GROUP)
        rows_x = pl.ds(pl.multiple_of(g * per_chunk, per_chunk), per_chunk)
        stack = jnp.concatenate([res[rows_x, a * back : (a + 1) * back] for a in range(chunks)], axis=0)
        out[rows_out, :] = jnp.dot(unsort, stack, preferred_element_type=jnp.float32).astype(jnp.bfloat16)

    done = pltpu.make_async_copy(out, out_hbm, out_sem)
    done.start()
    done.wait()


def ffn(c, wire, w_gate, w_up, w_down):
    rows, back = EXPERTS * c, c * UNIT // 2
    wire_rows = EXPERTS * 8
    any_spec = pl.BlockSpec(memory_space=pl.ANY)
    return pl.pallas_call(
        functools.partial(ffn_kernel, c),
        in_specs=[pl.BlockSpec(memory_space=pltpu.VMEM)] + [any_spec] * 3,
        out_specs=any_spec,
        out_shape=jax.ShapeDtypeStruct((wire_rows, back), jnp.bfloat16),
        scratch_shapes=[
            pltpu.VMEM((D, FF), jnp.bfloat16),
            pltpu.VMEM((D, FF), jnp.bfloat16),
            pltpu.VMEM((FF, D), jnp.bfloat16),
            pltpu.VMEM((rows, 2 * D), jnp.bfloat16),
            pltpu.VMEM((rows, FF), jnp.bfloat16),
            pltpu.VMEM((rows, FF), jnp.bfloat16),
            pltpu.VMEM((rows, D), jnp.bfloat16),
            pltpu.VMEM((wire_rows, back), jnp.bfloat16),
            pltpu.SemaphoreType.DMA((3, 4)),
            pltpu.SemaphoreType.DMA,
        ],
        compiler_params=pltpu.CompilerParams(vmem_limit_bytes=54 * MIB),
        cost_estimate=pl.CostEstimate(
            flops=2 * rows * 5 * D * FF, bytes_accessed=3 * D * FF * 2, transcendentals=rows * FF
        ),
        name="expert_gradients",
    )(wire, w_gate, w_up, w_down)


def spread_weights(ids, weight, c, first):
    rows = iota((EXPERTS, TOK), 0)
    dense = jnp.zeros((EXPERTS, TOK), jnp.float32)
    for k in range(TOP):
        dense = dense + jnp.where(ids[k : k + 1, :] == rows, weight[k : k + 1, :], 0.0)
    high = dense.astype(jnp.bfloat16).astype(jnp.float32)
    wide = EXPERTS * c
    spread = one(iota((wide, EXPERTS), 0) // c == iota((wide, EXPERTS), 1)).astype(jnp.bfloat16)
    rank, high, low = (
        jnp.dot(spread, v.astype(jnp.bfloat16), preferred_element_type=jnp.float32)
        for v in (routes(ids), high, dense - high)
    )
    hit = rank == (iota((wide, TOK), 0) % c).astype(jnp.float32) + first
    pair = [jnp.where(hit, v, 0.0).T for v in (high, low)]
    return jnp.concatenate(pair, axis=0).astype(jnp.bfloat16)


def slot_rows(c, y_ref, rows_ref):
    sort, per_chunk, back = sorter(c), SRC * c, c * UNIT // 2
    for g in range(EXPERTS // SRC):
        part = jnp.dot(
            sort, y_ref[g * GROUP : (g + 1) * GROUP, :], preferred_element_type=jnp.float32
        ).astype(jnp.bfloat16)
        for a in range(8 // c):
            rows_ref[g * per_chunk : (g + 1) * per_chunk, a * back : (a + 1) * back] = part[
                a * per_chunk : (a + 1) * per_chunk
            ]


def first_combine_kernel(ids_ref, weight_ref, y_ref, sum_ref, late_ref, rows_ref):
    ids, weight = ids_ref[...], weight_ref[...]
    late_ref[...] = spread_weights(ids, weight, *PARTS[1])
    slot_rows(4, y_ref, rows_ref)
    four = spread_weights(ids, weight, *PARTS[0])
    for q in range(4):
        cols = slice(q * UNIT, (q + 1) * UNIT)
        total = jnp.dot(four, rows_ref[:, cols], preferred_element_type=jnp.float32)
        sum_ref[:, cols] = total[:TOK] + total[TOK:]


def last_combine_kernel(late_ref, sum_hbm, y_ref, out_ref, sums, rows_ref, sem):
    copy = pltpu.make_async_copy(sum_hbm, sums, sem)
    copy.start()
    slot_rows(2, y_ref, rows_ref)
    copy.wait()
    total = jnp.dot(late_ref[...], rows_ref[...], preferred_element_type=jnp.float32)
    out_ref[...] = (sums[...] + total[:TOK] + total[TOK:]).astype(jnp.bfloat16)


def first_combine(ids, weight, y):
    vmem = pl.BlockSpec(memory_space=pltpu.VMEM)
    c, late = PARTS[0][0], PARTS[1][0]
    return pl.pallas_call(
        first_combine_kernel,
        in_specs=[vmem] * 3,
        out_specs=(vmem, vmem),
        out_shape=(
            pltpu.HBM((TOK, D), jnp.float32),
            pltpu.VMEM((2 * TOK, EXPERTS * late), jnp.bfloat16),
        ),
        scratch_shapes=[pltpu.VMEM((EXPERTS * c, D), jnp.bfloat16)],
        compiler_params=pltpu.CompilerParams(vmem_limit_bytes=40 * MIB),
        cost_estimate=pl.CostEstimate(
            flops=2 * 2 * TOK * EXPERTS * c * D * 2, bytes_accessed=EXPERTS * c * D * 2, transcendentals=0
        ),
        name="combine_first_slots",
    )(ids, weight, y)


def last_combine(late, sums, y):
    vmem = pl.BlockSpec(memory_space=pltpu.VMEM)
    c = PARTS[1][0]
    return pl.pallas_call(
        last_combine_kernel,
        in_specs=[vmem, pl.BlockSpec(memory_space=pl.ANY), vmem],
        out_specs=vmem,
        out_shape=jax.ShapeDtypeStruct((TOK, D), jnp.bfloat16),
        scratch_shapes=[
            pltpu.VMEM((TOK, D), jnp.float32),
            pltpu.VMEM((EXPERTS * c, D), jnp.bfloat16),
            pltpu.SemaphoreType.DMA,
        ],
        compiler_params=pltpu.CompilerParams(vmem_limit_bytes=20 * MIB),
        cost_estimate=pl.CostEstimate(
            flops=2 * 2 * TOK * EXPERTS * c * D * 2, bytes_accessed=EXPERTS * c * D * 2, transcendentals=0
        ),
        name="combine_last_slots",
    )(late, in_hbm(sums), y)


def exchange(wire):
    blocks = wire.reshape(EXPERTS, 8, wire.shape[1])
    return lax.all_to_all(blocks, AXES, split_axis=0, concat_axis=0, tiled=True).reshape(wire.shape)


def shards(tokens, grad_out, expert_ids, gate_weights, w_gate, w_up, w_down):
    w_gate, w_up, w_down = w_gate[0], w_up[0], w_down[0]
    ids, weights = expert_ids.T, gate_weights.T
    returned = []
    for (c, _), wire in zip(PARTS, pack(ids, tokens, grad_out)):
        returned.append(exchange(ffn(c, exchange(wire), w_gate, w_up, w_down)))
    sums, late = first_combine(ids, weights, returned[0])
    return last_combine(late, sums, returned[1])


def solution(mesh):
    rows = P(AXES, None)
    experts = P(AXES, None, None)
    return jax.shard_map(
        shards,
        mesh=mesh,
        in_specs=(rows, rows, rows, rows, experts, experts, experts),
        out_specs=rows,
        check_vma=False,
    )
```

```python
import functools

import jax
import jax.numpy as jnp
from jax import lax
from jax.experimental import pallas as pl
from jax.experimental.pallas import tpu as pltpu
from jax.sharding import PartitionSpec as P

AXES = ("node", "local")
D = 3584
FF = 1024
TOP = 8
TOK = 128
EXPERTS = 128
UNIT = 896
GROUP = 256
BLOCK = 512
SRC = 32
MIB = 1 << 20

PARTS = ((4, 0), (2, 4))


def iota(shape, dim):
    return lax.broadcasted_iota(jnp.int32, shape, dim)


def one(mask):
    return jnp.where(mask, 1.0, 0.0)


def routes(ids):
    rows = iota((EXPERTS, TOK), 0)
    chosen = jnp.zeros((EXPERTS, TOK), jnp.float32)
    for k in range(TOP):
        chosen = chosen + one(ids[k : k + 1, :] == rows)
    earlier = one(iota((TOK, TOK), 0) < iota((TOK, TOK), 1))
    rank = jnp.dot(
        chosen.astype(jnp.bfloat16), earlier.astype(jnp.bfloat16), preferred_element_type=jnp.float32
    )
    return jnp.where(chosen > 0.5, rank, 64.0)


def pack_kernel(ids_hbm, tokens_hbm, grads_hbm, *refs):
    out_refs, (ids, x, sems) = refs[: len(PARTS)], refs[len(PARTS) :]

    load_ids = pltpu.make_async_copy(ids_hbm, ids, sems.at[2])
    load_ids.start()
    loads = (
        pltpu.make_async_copy(tokens_hbm, x.at[pl.ds(0, TOK), :], sems.at[0]),
        pltpu.make_async_copy(grads_hbm, x.at[pl.ds(TOK, TOK), :], sems.at[1]),
    )
    for copy in loads:
        copy.start()

    load_ids.wait()
    ranks = routes(ids[...]).astype(jnp.bfloat16)
    spread = one(iota((BLOCK, BLOCK // 8), 0) >> 3 == iota((BLOCK, BLOCK // 8), 1)).astype(jnp.bfloat16)
    r = iota((BLOCK, TOK), 0) & 7
    blocks = EXPERTS * 8 // BLOCK

    def onehot(g, c, first):
        rank = ranks[g * BLOCK // 8 : (g + 1) * BLOCK // 8, :]
        rank = jnp.dot(spread, rank, preferred_element_type=jnp.float32)
        slot = (r & (c - 1)).astype(jnp.float32) + first
        chunk = jnp.where(rank == slot, r // c, -1)
        return jnp.concatenate([one(chunk == a).astype(jnp.bfloat16) for a in range(8 // c)], axis=1)

    def store(out_ref, g, hits, rows):
        out_ref[g * BLOCK : (g + 1) * BLOCK, :] = jnp.dot(
            hits, rows, preferred_element_type=jnp.float32
        ).astype(jnp.bfloat16)

    hits = onehot(0, *PARTS[0])
    for copy in loads:
        copy.wait()
    for g in range(blocks):
        store(out_refs[0], g, hits if g == 0 else onehot(g, *PARTS[0]), x[...])
    half = D // 2
    for g in range(blocks):
        stack = [x[:TOK, :half], x[:TOK, half:], x[TOK:, :half], x[TOK:, half:]]
        store(out_refs[1], g, onehot(g, *PARTS[1]), jnp.concatenate(stack, axis=0))


def in_hbm(v):
    return pltpu.with_memory_space_constraint(v, pltpu.HBM)


def pack(ids, tokens, grads):
    rows = EXPERTS * 8
    any_spec, vmem = pl.BlockSpec(memory_space=pl.ANY), pl.BlockSpec(memory_space=pltpu.VMEM)
    return pl.pallas_call(
        pack_kernel,
        in_specs=[any_spec] * 3,
        out_specs=[vmem for _ in PARTS],
        out_shape=[jax.ShapeDtypeStruct((rows, c * UNIT), jnp.bfloat16) for c, _ in PARTS],
        scratch_shapes=[
            pltpu.VMEM((TOP, TOK), jnp.int32),
            pltpu.VMEM((2 * TOK, D), jnp.bfloat16),
            pltpu.SemaphoreType.DMA((3,)),
        ],
        compiler_params=pltpu.CompilerParams(vmem_limit_bytes=24 * MIB),
        cost_estimate=pl.CostEstimate(
            flops=4 * rows * 2 * TOK * D, bytes_accessed=rows * 6 * UNIT * 2, transcendentals=0
        ),
        name="pack_slots",
    )(in_hbm(ids), in_hbm(tokens), in_hbm(grads))


def sorter(c):
    row, col = iota((GROUP, GROUP), 0), iota((GROUP, GROUP), 1)
    per_chunk = SRC * c
    inner = row % per_chunk
    return one(col == inner // c * 8 + row // per_chunk * c + inner % c).astype(jnp.bfloat16)


def unsorter(c):
    row, col = iota((GROUP, GROUP), 1), iota((GROUP, GROUP), 0)
    per_chunk = SRC * c
    inner = row % per_chunk
    return one(col == inner // c * 8 + row // per_chunk * c + inner % c).astype(jnp.bfloat16)


def ffn_kernel(c, wire_ref, wg_hbm, wu_hbm, wd_hbm, *refs):
    out_hbm, wg, wu, wd, x, up_g, gate_g, res, out, sems, out_sem = refs
    chunks, per_chunk = 8 // c, SRC * c
    width = c * UNIT
    step = 256
    blocks = FF // step

    def loads(j):
        cols = pl.ds(pl.multiple_of(j * step, step), step)
        return (
            pltpu.make_async_copy(wg_hbm.at[:, cols], wg.at[:, cols], sems.at[0, j]),
            pltpu.make_async_copy(wu_hbm.at[:, cols], wu.at[:, cols], sems.at[1, j]),
            pltpu.make_async_copy(wd_hbm.at[cols, :], wd.at[cols, :], sems.at[2, j]),
        )

    for j in range(blocks):
        for copy in loads(j):
            copy.start()

    sort = sorter(c)

    @pl.loop(0, EXPERTS // SRC)
    def _(g):
        rows_in = pl.ds(pl.multiple_of(g * GROUP, GROUP), GROUP)
        rows_x = pl.ds(pl.multiple_of(g * per_chunk, per_chunk), per_chunk)
        for u in range(c):
            part = jnp.dot(
                sort, wire_ref[rows_in, u * UNIT : (u + 1) * UNIT], preferred_element_type=jnp.float32
            ).astype(jnp.bfloat16)
            for a in range(chunks):
                at = a * width + u * UNIT
                x[rows_x, at : at + UNIT] = part[a * per_chunk : (a + 1) * per_chunk]

    @pl.loop(0, blocks)
    def _(j):
        for copy in loads(j):
            copy.wait()
        cols = pl.ds(pl.multiple_of(j * step, step), step)
        gate_pre = jnp.dot(x[:, :D], wg[:, cols], preferred_element_type=jnp.float32)
        up_pre = jnp.dot(x[:, :D], wu[:, cols], preferred_element_type=jnp.float32)
        hidden = lax.dot_general(
            x[:, D:], wd[cols, :], (((1,), (1,)), ((), ())), preferred_element_type=jnp.float32
        )
        s = jax.nn.sigmoid(gate_pre)
        up_g[:, cols] = (hidden * gate_pre * s).astype(jnp.bfloat16)
        gate_g[:, cols] = (hidden * up_pre * s * (1.0 + gate_pre * (1.0 - s))).astype(jnp.bfloat16)

    @pl.loop(0, D // 512)
    def _(j):
        cols = pl.ds(pl.multiple_of(j * 512, 512), 512)
        nt = (((1,), (1,)), ((), ()))
        total = lax.dot_general(gate_g[...], wg[cols, :], nt, preferred_element_type=jnp.float32)
        total = total + lax.dot_general(up_g[...], wu[cols, :], nt, preferred_element_type=jnp.float32)
        res[:, cols] = total.astype(jnp.bfloat16)

    unsort = unsorter(c)
    back = width // 2

    @pl.loop(0, EXPERTS // SRC)
    def _(g):
        rows_out = pl.ds(pl.multiple_of(g * GROUP, GROUP), GROUP)
        rows_x = pl.ds(pl.multiple_of(g * per_chunk, per_chunk), per_chunk)
        stack = jnp.concatenate([res[rows_x, a * back : (a + 1) * back] for a in range(chunks)], axis=0)
        out[rows_out, :] = jnp.dot(unsort, stack, preferred_element_type=jnp.float32).astype(jnp.bfloat16)

    done = pltpu.make_async_copy(out, out_hbm, out_sem)
    done.start()
    done.wait()


def ffn(c, wire, w_gate, w_up, w_down):
    rows, back = EXPERTS * c, c * UNIT // 2
    wire_rows = EXPERTS * 8
    any_spec = pl.BlockSpec(memory_space=pl.ANY)
    return pl.pallas_call(
        functools.partial(ffn_kernel, c),
        in_specs=[pl.BlockSpec(memory_space=pltpu.VMEM)] + [any_spec] * 3,
        out_specs=any_spec,
        out_shape=jax.ShapeDtypeStruct((wire_rows, back), jnp.bfloat16),
        scratch_shapes=[
            pltpu.VMEM((D, FF), jnp.bfloat16),
            pltpu.VMEM((D, FF), jnp.bfloat16),
            pltpu.VMEM((FF, D), jnp.bfloat16),
            pltpu.VMEM((rows, 2 * D), jnp.bfloat16),
            pltpu.VMEM((rows, FF), jnp.bfloat16),
            pltpu.VMEM((rows, FF), jnp.bfloat16),
            pltpu.VMEM((rows, D), jnp.bfloat16),
            pltpu.VMEM((wire_rows, back), jnp.bfloat16),
            pltpu.SemaphoreType.DMA((3, 4)),
            pltpu.SemaphoreType.DMA,
        ],
        compiler_params=pltpu.CompilerParams(vmem_limit_bytes=54 * MIB),
        cost_estimate=pl.CostEstimate(
            flops=2 * rows * 5 * D * FF, bytes_accessed=3 * D * FF * 2, transcendentals=rows * FF
        ),
        name="expert_gradients",
    )(wire, w_gate, w_up, w_down)


def spread_weights(ids, weight, c, first):
    rows = iota((EXPERTS, TOK), 0)
    dense = jnp.zeros((EXPERTS, TOK), jnp.float32)
    for k in range(TOP):
        dense = dense + jnp.where(ids[k : k + 1, :] == rows, weight[k : k + 1, :], 0.0)
    high = dense.astype(jnp.bfloat16).astype(jnp.float32)
    wide = EXPERTS * c
    spread = one(iota((wide, EXPERTS), 0) // c == iota((wide, EXPERTS), 1)).astype(jnp.bfloat16)
    rank, high, low = (
        jnp.dot(spread, v.astype(jnp.bfloat16), preferred_element_type=jnp.float32)
        for v in (routes(ids), high, dense - high)
    )
    hit = rank == (iota((wide, TOK), 0) % c).astype(jnp.float32) + first
    pair = [jnp.where(hit, v, 0.0).T for v in (high, low)]
    return jnp.concatenate(pair, axis=0).astype(jnp.bfloat16)


def slot_rows(c, y_ref, rows_ref):
    sort, per_chunk, back = sorter(c), SRC * c, c * UNIT // 2
    for g in range(EXPERTS // SRC):
        part = jnp.dot(
            sort, y_ref[g * GROUP : (g + 1) * GROUP, :], preferred_element_type=jnp.float32
        ).astype(jnp.bfloat16)
        for a in range(8 // c):
            rows_ref[g * per_chunk : (g + 1) * per_chunk, a * back : (a + 1) * back] = part[
                a * per_chunk : (a + 1) * per_chunk
            ]


def first_combine_kernel(ids_ref, weight_ref, y_ref, sum_ref, late_ref, rows_ref):
    ids, weight = ids_ref[...], weight_ref[...]
    late_ref[...] = spread_weights(ids, weight, *PARTS[1])
    slot_rows(4, y_ref, rows_ref)
    four = spread_weights(ids, weight, *PARTS[0])
    for q in range(4):
        cols = slice(q * UNIT, (q + 1) * UNIT)
        total = jnp.dot(four, rows_ref[:, cols], preferred_element_type=jnp.float32)
        sum_ref[:, cols] = total[:TOK] + total[TOK:]


def last_combine_kernel(late_hbm, sum_hbm, y_ref, out_hbm, late, sums, rows_ref, out, sems):
    halves = [pl.ds(h * D // 2, D // 2) for h in range(2)]
    load_late = pltpu.make_async_copy(late_hbm, late, sems.at[0])
    loads = [
        pltpu.make_async_copy(sum_hbm.at[:, cols], sums.at[:, cols], sems.at[1 + h])
        for h, cols in enumerate(halves)
    ]
    for copy in (load_late, *loads):
        copy.start()
    slot_rows(PARTS[1][0], y_ref, rows_ref)
    load_late.wait()
    stores = []
    for h, cols in enumerate(halves):
        total = jnp.dot(late[...], rows_ref[:, cols], preferred_element_type=jnp.float32)
        loads[h].wait()
        out[:, cols] = (sums[:, cols] + total[:TOK] + total[TOK:]).astype(jnp.bfloat16)
        stores.append(pltpu.make_async_copy(out.at[:, cols], out_hbm.at[:, cols], sems.at[3 + h]))
        stores[-1].start()
    for copy in stores:
        copy.wait()


def first_combine(ids, weight, y):
    vmem = pl.BlockSpec(memory_space=pltpu.VMEM)
    c, late = PARTS[0][0], PARTS[1][0]
    return pl.pallas_call(
        first_combine_kernel,
        in_specs=[vmem] * 3,
        out_specs=(vmem, vmem),
        out_shape=(
            pltpu.HBM((TOK, D), jnp.float32),
            pltpu.HBM((2 * TOK, EXPERTS * late), jnp.bfloat16),
        ),
        scratch_shapes=[pltpu.VMEM((EXPERTS * c, D), jnp.bfloat16)],
        compiler_params=pltpu.CompilerParams(vmem_limit_bytes=40 * MIB),
        cost_estimate=pl.CostEstimate(
            flops=2 * 2 * TOK * EXPERTS * c * D * 2, bytes_accessed=EXPERTS * c * D * 2, transcendentals=0
        ),
        name="combine_first_slots",
    )(ids, weight, y)


def last_combine(late, sums, y):
    any_spec, vmem = pl.BlockSpec(memory_space=pl.ANY), pl.BlockSpec(memory_space=pltpu.VMEM)
    c = PARTS[1][0]
    return pl.pallas_call(
        last_combine_kernel,
        in_specs=[any_spec, any_spec, vmem],
        out_specs=any_spec,
        out_shape=jax.ShapeDtypeStruct((TOK, D), jnp.bfloat16),
        scratch_shapes=[
            pltpu.VMEM((2 * TOK, EXPERTS * c), jnp.bfloat16),
            pltpu.VMEM((TOK, D), jnp.float32),
            pltpu.VMEM((EXPERTS * c, D), jnp.bfloat16),
            pltpu.VMEM((TOK, D), jnp.bfloat16),
            pltpu.SemaphoreType.DMA((5,)),
        ],
        compiler_params=pltpu.CompilerParams(vmem_limit_bytes=20 * MIB),
        cost_estimate=pl.CostEstimate(
            flops=2 * 2 * TOK * EXPERTS * c * D * 2, bytes_accessed=EXPERTS * c * D * 2, transcendentals=0
        ),
        name="combine_last_slots",
    )(in_hbm(late), in_hbm(sums), y)


def exchange(wire):
    blocks = wire.reshape(EXPERTS, 8, wire.shape[1])
    return lax.all_to_all(blocks, AXES, split_axis=0, concat_axis=0, tiled=True).reshape(wire.shape)


def shards(tokens, grad_out, expert_ids, gate_weights, w_gate, w_up, w_down):
    w_gate, w_up, w_down = w_gate[0], w_up[0], w_down[0]
    ids, weights = expert_ids.T, gate_weights.T
    returned = []
    for (c, _), wire in zip(PARTS, pack(ids, tokens, grad_out)):
        returned.append(exchange(ffn(c, exchange(wire), w_gate, w_up, w_down)))
    sums, late = first_combine(ids, weights, returned[0])
    return last_combine(late, sums, returned[1])


def solution(mesh):
    rows = P(AXES, None)
    experts = P(AXES, None, None)
    return jax.shard_map(
        shards,
        mesh=mesh,
        in_specs=(rows, rows, rows, rows, experts, experts, experts),
        out_specs=rows,
        check_vma=False,
    )
```

```python
import functools

import jax
import jax.numpy as jnp
from jax import lax
from jax.experimental import pallas as pl
from jax.experimental.pallas import tpu as pltpu
from jax.sharding import PartitionSpec as P

AXES = ("node", "local")
D = 3584
FF = 1024
TOP = 8
TOK = 128
EXPERTS = 128
UNIT = 896
GROUP = 256
BLOCK = 512
SRC = 32
MIB = 1 << 20

PARTS = ((4, 0), (2, 4))


def iota(shape, dim):
    return lax.broadcasted_iota(jnp.int32, shape, dim)


def one(mask):
    return jnp.where(mask, 1.0, 0.0)


def routes(ids):
    rows = iota((EXPERTS, TOK), 0)
    chosen = jnp.zeros((EXPERTS, TOK), jnp.float32)
    for k in range(TOP):
        chosen = chosen + one(ids[k : k + 1, :] == rows)
    earlier = one(iota((TOK, TOK), 0) < iota((TOK, TOK), 1))
    rank = jnp.dot(
        chosen.astype(jnp.bfloat16), earlier.astype(jnp.bfloat16), preferred_element_type=jnp.float32
    )
    return jnp.where(chosen > 0.5, rank, 64.0)


def pack_kernel(ids_hbm, tokens_hbm, grads_hbm, *refs):
    out_refs, (ids, x, sems) = refs[: len(PARTS)], refs[len(PARTS) :]

    load_ids = pltpu.make_async_copy(ids_hbm, ids, sems.at[2])
    load_ids.start()
    loads = (
        pltpu.make_async_copy(tokens_hbm, x.at[pl.ds(0, TOK), :], sems.at[0]),
        pltpu.make_async_copy(grads_hbm, x.at[pl.ds(TOK, TOK), :], sems.at[1]),
    )
    for copy in loads:
        copy.start()

    load_ids.wait()
    ranks = routes(ids[...]).astype(jnp.bfloat16)
    spread = one(iota((BLOCK, BLOCK // 8), 0) >> 3 == iota((BLOCK, BLOCK // 8), 1)).astype(jnp.bfloat16)
    r = iota((BLOCK, TOK), 0) & 7
    blocks = EXPERTS * 8 // BLOCK

    def onehot(g, c, first):
        rank = ranks[g * BLOCK // 8 : (g + 1) * BLOCK // 8, :]
        rank = jnp.dot(spread, rank, preferred_element_type=jnp.float32)
        slot = (r & (c - 1)).astype(jnp.float32) + first
        chunk = jnp.where(rank == slot, r // c, -1)
        return jnp.concatenate([one(chunk == a).astype(jnp.bfloat16) for a in range(8 // c)], axis=1)

    def store(out_ref, g, hits, rows):
        out_ref[g * BLOCK : (g + 1) * BLOCK, :] = jnp.dot(
            hits, rows, preferred_element_type=jnp.float32
        ).astype(jnp.bfloat16)

    hits = onehot(0, *PARTS[0])
    for copy in loads:
        copy.wait()
    for g in range(blocks):
        store(out_refs[0], g, hits if g == 0 else onehot(g, *PARTS[0]), x[...])
    half = D // 2
    for g in range(blocks):
        stack = [x[:TOK, :half], x[:TOK, half:], x[TOK:, :half], x[TOK:, half:]]
        store(out_refs[1], g, onehot(g, *PARTS[1]), jnp.concatenate(stack, axis=0))


def in_hbm(v):
    return pltpu.with_memory_space_constraint(v, pltpu.HBM)


def pack(ids, tokens, grads):
    rows = EXPERTS * 8
    any_spec, vmem = pl.BlockSpec(memory_space=pl.ANY), pl.BlockSpec(memory_space=pltpu.VMEM)
    return pl.pallas_call(
        pack_kernel,
        in_specs=[any_spec] * 3,
        out_specs=[vmem for _ in PARTS],
        out_shape=[jax.ShapeDtypeStruct((rows, c * UNIT), jnp.bfloat16) for c, _ in PARTS],
        scratch_shapes=[
            pltpu.VMEM((TOP, TOK), jnp.int32),
            pltpu.VMEM((2 * TOK, D), jnp.bfloat16),
            pltpu.SemaphoreType.DMA((3,)),
        ],
        compiler_params=pltpu.CompilerParams(vmem_limit_bytes=24 * MIB),
        cost_estimate=pl.CostEstimate(
            flops=4 * rows * 2 * TOK * D, bytes_accessed=rows * 6 * UNIT * 2, transcendentals=0
        ),
        name="pack_slots",
    )(in_hbm(ids), in_hbm(tokens), in_hbm(grads))


def sorter(c):
    row, col = iota((GROUP, GROUP), 0), iota((GROUP, GROUP), 1)
    per_chunk = SRC * c
    inner = row % per_chunk
    return one(col == inner // c * 8 + row // per_chunk * c + inner % c).astype(jnp.bfloat16)


def unsorter(c):
    row, col = iota((GROUP, GROUP), 1), iota((GROUP, GROUP), 0)
    per_chunk = SRC * c
    inner = row % per_chunk
    return one(col == inner // c * 8 + row // per_chunk * c + inner % c).astype(jnp.bfloat16)


def ffn_kernel(c, wire_ref, wg_hbm, wu_hbm, wd_hbm, *refs):
    out_hbm, wg, wu, wd, x, up_g, gate_g, res, out, sems, out_sem = refs
    chunks, per_chunk = 8 // c, SRC * c
    width = c * UNIT
    step = 256
    blocks = FF // step

    def loads(j):
        cols = pl.ds(pl.multiple_of(j * step, step), step)
        return (
            pltpu.make_async_copy(wg_hbm.at[:, cols], wg.at[:, cols], sems.at[0, j]),
            pltpu.make_async_copy(wu_hbm.at[:, cols], wu.at[:, cols], sems.at[1, j]),
            pltpu.make_async_copy(wd_hbm.at[cols, :], wd.at[cols, :], sems.at[2, j]),
        )

    for j in range(blocks):
        for copy in loads(j):
            copy.start()

    sort = sorter(c)

    @pl.loop(0, EXPERTS // SRC)
    def _(g):
        rows_in = pl.ds(pl.multiple_of(g * GROUP, GROUP), GROUP)
        rows_x = pl.ds(pl.multiple_of(g * per_chunk, per_chunk), per_chunk)
        for u in range(c):
            part = jnp.dot(
                sort, wire_ref[rows_in, u * UNIT : (u + 1) * UNIT], preferred_element_type=jnp.float32
            ).astype(jnp.bfloat16)
            for a in range(chunks):
                at = a * width + u * UNIT
                x[rows_x, at : at + UNIT] = part[a * per_chunk : (a + 1) * per_chunk]

    @pl.loop(0, blocks)
    def _(j):
        for copy in loads(j):
            copy.wait()
        cols = pl.ds(pl.multiple_of(j * step, step), step)
        gate_pre = jnp.dot(x[:, :D], wg[:, cols], preferred_element_type=jnp.float32)
        up_pre = jnp.dot(x[:, :D], wu[:, cols], preferred_element_type=jnp.float32)
        hidden = lax.dot_general(
            x[:, D:], wd[cols, :], (((1,), (1,)), ((), ())), preferred_element_type=jnp.float32
        )
        s = jax.nn.sigmoid(gate_pre)
        up_g[:, cols] = (hidden * gate_pre * s).astype(jnp.bfloat16)
        gate_g[:, cols] = (hidden * up_pre * s * (1.0 + gate_pre * (1.0 - s))).astype(jnp.bfloat16)

    @pl.loop(0, D // 512)
    def _(j):
        cols = pl.ds(pl.multiple_of(j * 512, 512), 512)
        nt = (((1,), (1,)), ((), ()))
        total = lax.dot_general(gate_g[...], wg[cols, :], nt, preferred_element_type=jnp.float32)
        total = total + lax.dot_general(up_g[...], wu[cols, :], nt, preferred_element_type=jnp.float32)
        res[:, cols] = total.astype(jnp.bfloat16)

    unsort = unsorter(c)
    back = width // 2

    @pl.loop(0, EXPERTS // SRC)
    def _(g):
        rows_out = pl.ds(pl.multiple_of(g * GROUP, GROUP), GROUP)
        rows_x = pl.ds(pl.multiple_of(g * per_chunk, per_chunk), per_chunk)
        stack = jnp.concatenate([res[rows_x, a * back : (a + 1) * back] for a in range(chunks)], axis=0)
        out[rows_out, :] = jnp.dot(unsort, stack, preferred_element_type=jnp.float32).astype(jnp.bfloat16)

    done = pltpu.make_async_copy(out, out_hbm, out_sem)
    done.start()
    done.wait()


def ffn(c, wire, w_gate, w_up, w_down):
    rows, back = EXPERTS * c, c * UNIT // 2
    wire_rows = EXPERTS * 8
    any_spec = pl.BlockSpec(memory_space=pl.ANY)
    return pl.pallas_call(
        functools.partial(ffn_kernel, c),
        in_specs=[pl.BlockSpec(memory_space=pltpu.VMEM)] + [any_spec] * 3,
        out_specs=any_spec,
        out_shape=jax.ShapeDtypeStruct((wire_rows, back), jnp.bfloat16),
        scratch_shapes=[
            pltpu.VMEM((D, FF), jnp.bfloat16),
            pltpu.VMEM((D, FF), jnp.bfloat16),
            pltpu.VMEM((FF, D), jnp.bfloat16),
            pltpu.VMEM((rows, 2 * D), jnp.bfloat16),
            pltpu.VMEM((rows, FF), jnp.bfloat16),
            pltpu.VMEM((rows, FF), jnp.bfloat16),
            pltpu.VMEM((rows, D), jnp.bfloat16),
            pltpu.VMEM((wire_rows, back), jnp.bfloat16),
            pltpu.SemaphoreType.DMA((3, 4)),
            pltpu.SemaphoreType.DMA,
        ],
        compiler_params=pltpu.CompilerParams(vmem_limit_bytes=54 * MIB),
        cost_estimate=pl.CostEstimate(
            flops=2 * rows * 5 * D * FF, bytes_accessed=3 * D * FF * 2, transcendentals=rows * FF
        ),
        name="expert_gradients",
    )(wire, w_gate, w_up, w_down)


def spread_weights(ids, weight, c, first):
    rows = iota((EXPERTS, TOK), 0)
    dense = jnp.zeros((EXPERTS, TOK), jnp.float32)
    for k in range(TOP):
        dense = dense + jnp.where(ids[k : k + 1, :] == rows, weight[k : k + 1, :], 0.0)
    high = dense.astype(jnp.bfloat16).astype(jnp.float32)
    wide = EXPERTS * c
    spread = one(iota((wide, EXPERTS), 0) // c == iota((wide, EXPERTS), 1)).astype(jnp.bfloat16)
    rank, high, low = (
        jnp.dot(spread, v.astype(jnp.bfloat16), preferred_element_type=jnp.float32)
        for v in (routes(ids), high, dense - high)
    )
    hit = rank == (iota((wide, TOK), 0) % c).astype(jnp.float32) + first
    pair = [jnp.where(hit, v, 0.0).T for v in (high, low)]
    return jnp.concatenate(pair, axis=0).astype(jnp.bfloat16)


def slot_rows(c, y_ref, rows_ref):
    sort, per_chunk, back = sorter(c), SRC * c, c * UNIT // 2
    for g in range(EXPERTS // SRC):
        part = jnp.dot(
            sort, y_ref[g * GROUP : (g + 1) * GROUP, :], preferred_element_type=jnp.float32
        ).astype(jnp.bfloat16)
        for a in range(8 // c):
            rows_ref[g * per_chunk : (g + 1) * per_chunk, a * back : (a + 1) * back] = part[
                a * per_chunk : (a + 1) * per_chunk
            ]


def first_combine_kernel(ids_ref, weight_ref, y_ref, sum_ref, late_ref, rows_ref):
    ids, weight = ids_ref[...], weight_ref[...]
    late_ref[...] = spread_weights(ids, weight, *PARTS[1])
    slot_rows(4, y_ref, rows_ref)
    four = spread_weights(ids, weight, *PARTS[0])
    for q in range(4):
        cols = slice(q * UNIT, (q + 1) * UNIT)
        total = jnp.dot(four, rows_ref[:, cols], preferred_element_type=jnp.float32)
        sum_ref[:, cols] = total[:TOK] + total[TOK:]


def last_combine_kernel(late_hbm, sum_hbm, y_ref, out_hbm, late, sums, rows_ref, out, sems):
    quarters = [pl.ds(q * UNIT, UNIT) for q in range(4)]
    load_late = pltpu.make_async_copy(late_hbm, late, sems.at[0])
    loads = [
        pltpu.make_async_copy(sum_hbm.at[:, cols], sums.at[:, cols], sems.at[1 + q])
        for q, cols in enumerate(quarters)
    ]
    for copy in (load_late, *loads):
        copy.start()
    slot_rows(PARTS[1][0], y_ref, rows_ref)
    load_late.wait()
    stores = []
    for q, cols in enumerate(quarters):
        total = jnp.dot(late[...], rows_ref[:, cols], preferred_element_type=jnp.float32)
        loads[q].wait()
        out[:, cols] = (sums[:, cols] + total[:TOK] + total[TOK:]).astype(jnp.bfloat16)
        stores.append(pltpu.make_async_copy(out.at[:, cols], out_hbm.at[:, cols], sems.at[5 + q]))
        stores[-1].start()
    for copy in stores:
        copy.wait()


def first_combine(ids, weight, y):
    vmem = pl.BlockSpec(memory_space=pltpu.VMEM)
    c, late = PARTS[0][0], PARTS[1][0]
    return pl.pallas_call(
        first_combine_kernel,
        in_specs=[vmem] * 3,
        out_specs=(vmem, vmem),
        out_shape=(
            pltpu.HBM((TOK, D), jnp.float32),
            pltpu.HBM((2 * TOK, EXPERTS * late), jnp.bfloat16),
        ),
        scratch_shapes=[pltpu.VMEM((EXPERTS * c, D), jnp.bfloat16)],
        compiler_params=pltpu.CompilerParams(vmem_limit_bytes=40 * MIB),
        cost_estimate=pl.CostEstimate(
            flops=2 * 2 * TOK * EXPERTS * c * D * 2, bytes_accessed=EXPERTS * c * D * 2, transcendentals=0
        ),
        name="combine_first_slots",
    )(ids, weight, y)


def last_combine(late, sums, y):
    any_spec, vmem = pl.BlockSpec(memory_space=pl.ANY), pl.BlockSpec(memory_space=pltpu.VMEM)
    c = PARTS[1][0]
    return pl.pallas_call(
        last_combine_kernel,
        in_specs=[any_spec, any_spec, vmem],
        out_specs=any_spec,
        out_shape=jax.ShapeDtypeStruct((TOK, D), jnp.bfloat16),
        scratch_shapes=[
            pltpu.VMEM((2 * TOK, EXPERTS * c), jnp.bfloat16),
            pltpu.VMEM((TOK, D), jnp.float32),
            pltpu.VMEM((EXPERTS * c, D), jnp.bfloat16),
            pltpu.VMEM((TOK, D), jnp.bfloat16),
            pltpu.SemaphoreType.DMA((9,)),
        ],
        compiler_params=pltpu.CompilerParams(vmem_limit_bytes=20 * MIB),
        cost_estimate=pl.CostEstimate(
            flops=2 * 2 * TOK * EXPERTS * c * D * 2, bytes_accessed=EXPERTS * c * D * 2, transcendentals=0
        ),
        name="combine_last_slots",
    )(in_hbm(late), in_hbm(sums), y)


def exchange(wire):
    blocks = wire.reshape(EXPERTS, 8, wire.shape[1])
    return lax.all_to_all(blocks, AXES, split_axis=0, concat_axis=0, tiled=True).reshape(wire.shape)


def shards(tokens, grad_out, expert_ids, gate_weights, w_gate, w_up, w_down):
    w_gate, w_up, w_down = w_gate[0], w_up[0], w_down[0]
    ids, weights = expert_ids.T, gate_weights.T
    returned = []
    for (c, _), wire in zip(PARTS, pack(ids, tokens, grad_out)):
        returned.append(exchange(ffn(c, exchange(wire), w_gate, w_up, w_down)))
    sums, late = first_combine(ids, weights, returned[0])
    return last_combine(late, sums, returned[1])


def solution(mesh):
    rows = P(AXES, None)
    experts = P(AXES, None, None)
    return jax.shard_map(
        shards,
        mesh=mesh,
        in_specs=(rows, rows, rows, rows, experts, experts, experts),
        out_specs=rows,
        check_vma=False,
    )
```
